32 devices in a mesh: parts: 2 (over y), grid: 4 (over z), dom: 4 (over x, core).
Axes of the slice: x: 2, y: 2, z: 4, core: 2. Of those that a mesh axis runs over, the one named last changes fastest.
Arguments:
- initial: float32 [8, 512, 4, 128], P(('parts', 'grid'), None, 'dom'), parts along dimension 0, may hold values from -6 to 6
- levels: int32 [8, 2], P(('parts', 'grid')), parts along dimension 0, may hold values from 1 to 7, as said below
- coefficients: int32 [8], P(('parts', 'grid')), parts along dimension 0, may hold values from -1 to 1, as said below
- velocity: float32 [8], P('parts'), parts along dimension 0, may hold values from -0.15 to 0.15
- position: int32 [1792], replicated, may hold values from 0 to 1791, each once
Outputs:
- combined: float32 [3584, 4, 128], P(('parts', 'grid'), 'dom'), parts along dimension 0
- result: float32 [8, 512, 4, 128], P(('parts', 'grid'), None, 'dom'), parts along dimension 0
The draws below stay inside these ranges and needn't reach their ends.
There are 2 independent parts, one for each index of `parts`. The reference program is written for one: setup_inputs(seed, part) draws one part's arguments, and reference() takes and returns one part's arrays. A program takes and returns all parts, laid end to end along the dimension named above; an argument that names none is the same for every part. Nothing has to cross between parts.
Inputs may be any that keep to these rules, and one draw needn't show every extreme that they name: `levels`: each row is (l1, l2) with l1 + l2 equal to 9 or 8, both at least 1 and l1 at least 2; grid 0 is (2, M - 2). `coefficients`: +1 for grids with l1 + l2 = 9, -1 for l1 + l2 = 8.
All inputs are finite; a program needn't handle non-finite values.
Results may differ from the reference program's by a relative error of at most 0.0003.
Values sent between devices are 32-bit elements; how exact they have to be, the bound alone decides.
A program may use at most 64 MiB of HBM per device.

```python
import jax
import jax.numpy as jnp
from jax import lax

M = 9
LMIN = 2
STEPS = 4
N4 = 128
NGRIDS = 4
PTS = 512
SP = 1792
N3 = 4


def grid_plan(key):
    on_upper = jax.random.randint(jax.random.fold_in(key, 11), (NGRIDS,), 0, 2)
    on_upper = on_upper.at[0].set(1).at[1].set(0)
    options = M - 2 * LMIN + 1 - (1 - on_upper)
    offset_pick = jax.random.randint(jax.random.fold_in(key, 12), (NGRIDS,), 0, 1 << 20) % options
    offset_pick = offset_pick.at[0].set(0)
    level_one = LMIN + offset_pick
    level_two = M - (1 - on_upper) - level_one
    return (level_one, level_two, on_upper)


def draw_levels(key, part):
    level_one, level_two, on_upper = grid_plan(key)
    return jnp.stack([level_one, level_two], axis=1).astype(jnp.int32)


def draw_coefficients(key, part):
    level_one, level_two, on_upper = grid_plan(key)
    return (2 * on_upper - 1).astype(jnp.int32)


def steps_of(stream_key, dims, split, least, high):
    factor_of = 1.0
    for dim, shards_of in split:
        steps = jax.random.uniform(jax.random.fold_in(jax.random.fold_in(stream_key, 6), dim), (shards_of,), jnp.float32, least / len(split), high / len(split))
        factor_of = factor_of * jnp.repeat(jnp.exp(steps), dims[dim] // shards_of).reshape((-1,) + (1,) * (len(dims) - 1 - dim))
    return factor_of


def noise(rng, shape, deviation, limit, cuts=(), held_as=jnp.bfloat16):
    values = jax.random.normal(rng, shape, jnp.float32) * deviation
    if len(cuts) > 0:
        values = steps_of(rng, shape, cuts, -0.22, 0.18) * values
    return jnp.clip(values, min=-limit, max=limit).astype(held_as)


def setup_inputs(seed: int = 0, part: int = 0) -> dict:
    key_list = jax.random.split(jax.random.key(seed), 6)
    own_keys = jax.random.split(jax.random.fold_in(key_list[5], part), 6)
    initial = noise(own_keys[0], (NGRIDS, PTS, N3, N4), 1.0, 6.0, ((0, 4), (2, 4)), jnp.float32)
    levels = draw_levels(jax.random.fold_in(jax.random.fold_in(key_list[5], part), 71), part)
    coefficients = draw_coefficients(jax.random.fold_in(jax.random.fold_in(key_list[5], part), 71), part)
    velocity = jnp.clip(jax.random.uniform(own_keys[3], (4,), jnp.float32, -0.15, 0.15), -0.15, 0.15)
    position = jax.random.permutation(key_list[4], SP).astype(jnp.int32)
    return dict(initial=initial, levels=levels, coefficients=coefficients, velocity=velocity, position=position)


DIFFUSE = 0.05


def grid_coords(level_one, level_two, count):
    flat_rows = jnp.arange(count, dtype=jnp.int32)
    size_one = jnp.left_shift(jnp.int32(1), level_one)
    size_two = jnp.left_shift(jnp.int32(1), level_two)
    inside = flat_rows < size_one * size_two
    along_one = jnp.minimum(flat_rows // size_two, size_one - 1)
    along_two = flat_rows % size_two
    return (flat_rows, inside, along_one, along_two, size_one, size_two, level_one, level_two)


def neighbour(geometry, which, offset):
    flat_rows, inside = geometry[0], geometry[1]
    if which == 0:
        coord, size, stride_rows = geometry[2], geometry[4], geometry[5]
    else:
        coord, size, stride_rows = geometry[3], geometry[5], 1
    moved = flat_rows + ((coord + offset) % size - coord) * stride_rows
    return jnp.where(inside, moved, flat_rows)


def advance(values, above, below, speeds, geometry):
    pairs = ((values[neighbour(geometry, 0, 1)], values[neighbour(geometry, 0, -1)]),
             (values[neighbour(geometry, 1, 1)], values[neighbour(geometry, 1, -1)]),
             (above, below),
             (jnp.roll(values, -1, axis=2), jnp.roll(values, 1, axis=2)))
    change = jnp.zeros_like(values)
    for axis_idx in range(4):
        ahead, behind = pairs[axis_idx]
        speed = speeds[axis_idx]
        change = change + DIFFUSE * (ahead - 2.0 * values + behind) - jnp.maximum(speed, 0.0) * (values - behind) - jnp.minimum(speed, 0.0) * (ahead - values)
    return jnp.where(geometry[1][:, None, None], values + change, 0.0)


def sweep(values, geometry, which, direction):
    flat_rows, inside = geometry[0], geometry[1]
    if which == 0:
        coord, size, stride_rows, level = geometry[2], geometry[4], geometry[5], geometry[6]
    else:
        coord, size, stride_rows, level = geometry[3], geometry[5], 1, geometry[7]
    order = list(range(M)) if direction < 0 else list(range(M - 1, -1, -1))
    for level_idx in order:
        stride = 1 << level_idx
        active = inside & (level_idx < level) & (coord % (2 * stride) == stride)
        ahead = jnp.where(active, flat_rows + ((coord + stride) % size - coord) * stride_rows, flat_rows)
        behind = jnp.where(active, flat_rows + ((coord - stride) % size - coord) * stride_rows, flat_rows)
        values = values + jnp.where(active[:, None, None], direction * 0.5 * (values[ahead] + values[behind]), 0.0)
    return values


def hier_index(coord, level):
    positive = coord > 0
    zeros_count = jnp.zeros_like(coord)
    for bit_idx in range(1, M + 1):
        zeros_count = zeros_count + (positive & (coord % (1 << bit_idx) == 0)).astype(jnp.int32)
    bit_level = level - zeros_count
    head = jnp.left_shift(jnp.int32(1), jnp.maximum(bit_level - 1, 0))
    return jnp.where(positive, head + jnp.right_shift(coord, zeros_count + 1), 0)


def sparse_rows(geometry, position):
    h_one = hier_index(geometry[2], geometry[6])
    h_two = hier_index(geometry[3], geometry[7])
    bit_count = jnp.zeros_like(h_one)
    for bit_idx in range(M):
        bit_count = bit_count + (h_one >= (1 << bit_idx)).astype(jnp.int32)
    low_part = h_one * (1 << (M - LMIN))
    high_part = (1 << M) + (bit_count - 1 - LMIN) * (1 << (M - 1)) + (h_one - jnp.left_shift(jnp.int32(1), jnp.maximum(bit_count - 1, 0))) * jnp.left_shift(jnp.int32(1), M - bit_count)
    sparse_id = jnp.where(bit_count <= LMIN, low_part, high_part) + h_two
    return jnp.where(geometry[1], position[jnp.minimum(sparse_id, SP - 1)], SP)


def reference(initial, levels, coefficients, velocity, position):
    def contribute(buffer, grid_item):
        start_values, level_pair, weight_sign = grid_item
        geometry = grid_coords(level_pair[0], level_pair[1], start_values.shape[0])
        values = jnp.where(geometry[1][:, None, None], start_values, 0.0)
        for time_idx in range(STEPS):
            values = advance(values, jnp.roll(values, -1, axis=1), jnp.roll(values, 1, axis=1), velocity, geometry)
        values = sweep(sweep(values, geometry, 1, -1.0), geometry, 0, -1.0)
        target_rows = sparse_rows(geometry, position)
        return buffer.at[target_rows].add(weight_sign.astype(jnp.float32) * values, mode="drop"), None

    buffer = jnp.zeros((SP,) + initial.shape[2:], jnp.float32)
    buffer, unused = lax.scan(contribute, buffer, (initial, levels, coefficients))

    def restore(level_pair):
        geometry = grid_coords(level_pair[0], level_pair[1], initial.shape[1])
        target_rows = sparse_rows(geometry, position)
        values = jnp.where(geometry[1][:, None, None], buffer[jnp.minimum(target_rows, SP - 1)], 0.0)
        return sweep(sweep(values, geometry, 0, 1.0), geometry, 1, 1.0)

    result = lax.map(restore, levels)
    return buffer, result
```

```python
import functools
from math import comb

import jax
import jax.numpy as jnp
from jax import lax
from jax.experimental import pallas as pl
from jax.experimental.pallas import tpu as pltpu
from jax.sharding import PartitionSpec as P

M = 9
LMIN = 2
STEPS = 4
DIFFUSE = 0.05
TOP = M - LMIN
UNIT = 1 << TOP
PIECES = 4
BLOCK = 64
MESH = pl.DeviceIdType.MESH
F32 = jnp.float32
BF16 = jnp.bfloat16


def coords(flat, level_one, level_two):
    one = jnp.left_shift(jnp.right_shift(flat, level_two), TOP - level_one)
    two = jnp.left_shift(flat & (jnp.left_shift(jnp.int32(1), level_two) - 1), TOP - level_two)
    return one, two


def trailing(coord):
    zeros = jnp.zeros_like(coord)
    for bit in range(1, TOP):
        zeros = zeros + jnp.where((coord & ((1 << bit) - 1)) == 0, 1, 0)
    return zeros


def inverse_width(coord, zeros):
    width = jnp.zeros(coord.shape, F32)
    for bit in range(TOP):
        width = jnp.where(zeros == bit, 0.5**bit, width)
    return jnp.where(coord == 0, 0.0, width)


def hier(coord, zeros):
    index = jnp.right_shift(jnp.full_like(coord, UNIT // 2), zeros)
    return jnp.where(coord == 0, 0, index + jnp.right_shift(coord, zeros + 1))


def sparse_ids(one, two, zeros_one, zeros_two):
    h_one, h_two = hier(one, zeros_one), hier(two, zeros_two)
    bits = jnp.where(one == 0, 0, TOP - zeros_one)
    head = jnp.left_shift(jnp.ones_like(one), jnp.maximum(bits - 1, 0))
    low = h_one * (1 << TOP)
    high = (1 << M) + (bits - 1 - LMIN) * (1 << (M - 1)) + (h_one - head) * jnp.left_shift(
        jnp.ones_like(one), M - bits
    )
    return jnp.where(bits <= LMIN, low, high) + h_two


def split(values):
    high = values.astype(BF16)
    low = (values - high.astype(F32)).astype(BF16)
    return jnp.concatenate([high, low], axis=1)


def product(matrix, values):
    width = values.shape[1]
    both = jnp.dot(matrix, split(values), preferred_element_type=F32)
    return both[:, :width] + both[:, width:]


def kernel(
    doms, grids, lev, coef, vel, pos, start, own_ref, result_ref,
    layers, fields, meta, basis, surplus_of, mats, total,
    layer_send, layer_recv, pass_send, meta_send, meta_recv, right_send, left_send, sur_recv,
):
    rows, lanes = start.shape
    owned = own_ref.shape[0]
    chips = doms // 2
    here = lax.axis_index("dom")
    z = lax.axis_index("grid")
    chip, core = here // 2, lax.rem(here, 2)
    sibling = here + 1 - 2 * core
    level_one, level_two = lev[0, 0], lev[0, 1]
    stride, live = jnp.int32(1), jnp.int32(rows)
    for level in range(1, TOP + 1):
        stride = jnp.where(level_two == level, 1 << level, stride)
    for level in range(M):
        live = jnp.where(level_one + level_two == level, 1 << level, live)

    others = [lax.rem(chip + j, chips) * 2 + core for j in range(1, chips)]
    sources = [lax.rem(chip + chips - j, chips) * 2 + core for j in range(1, chips)]
    peers = [lax.rem(z + j, grids) for j in range(1, grids)]

    barrier = pltpu.get_barrier_semaphore()
    for peer in [sibling] + others:
        pl.semaphore_signal(barrier, inc=1, device_id={"dom": peer}, device_id_type=MESH)
    for peer in peers:
        pl.semaphore_signal(barrier, inc=1, device_id={"grid": peer}, device_id_type=MESH)
    pl.semaphore_wait(barrier, chips + grids - 1)

    piece_rows = rows // PIECES

    def layer_copy(source, slot, piece, target, send):
        at = pl.ds(piece * piece_rows, piece_rows)
        return pltpu.make_async_remote_copy(
            src_ref=source.at[at],
            dst_ref=layers.at[slot, at],
            send_sem=send,
            recv_sem=layer_recv.at[slot, piece],
            device_id={"dom": target},
            device_id_type=MESH,
        )

    for piece in range(PIECES):
        for j, peer in enumerate(others):
            layer_copy(start, here, piece, peer, layer_send.at[j, piece]).start()
    for piece in range(PIECES):
        layer_copy(start, here, piece, sibling, layer_send.at[chips - 1, piece]).start()

    flat = lax.broadcasted_iota(jnp.int32, (1, rows), 1)
    one, two = coords(flat, level_one, level_two)
    zeros_one, zeros_two = trailing(one), trailing(two)
    ids = jnp.where(flat < live, sparse_ids(one, two, zeros_one, zeros_two), -1)
    lines = [
        one.astype(F32), two.astype(F32),
        inverse_width(one, zeros_one), inverse_width(two, zeros_two),
        ids.astype(F32),
    ]
    for line, value in enumerate(lines):
        meta[z, line : line + 1, :] = value
    meta[z, len(lines) :, :] = jnp.zeros((8 - len(lines), rows), F32)

    def meta_copy(j):
        return pltpu.make_async_remote_copy(
            src_ref=meta.at[z],
            dst_ref=meta.at[z],
            send_sem=meta_send.at[j],
            recv_sem=meta_recv.at[z],
            device_id={"grid": peers[j]},
            device_id_type=MESH,
        )

    for j in range(grids - 1):
        meta_copy(j).start()

    def pass_on(piece):
        for j, slot in enumerate(sources):
            layer_copy(start, slot, piece, sibling, layer_send.at[0, 0]).wait_recv()
            layer_copy(layers.at[slot], slot, piece, sibling, pass_send.at[j, piece]).start()

    def column(begin, count):
        return begin + lax.broadcasted_iota(jnp.int32, (count, 1), 0)

    def build_basis(step, carry):
        begin = pl.multiple_of(step * BLOCK, BLOCK)
        row_one, row_two = coords(column(begin, BLOCK), level_one, level_two)

        def factor(row, col):
            width = jnp.where(row == 0, 2 * UNIT - 1, row & (-row))
            apart = (col - row) & (UNIT - 1)
            near = jnp.where(apart == 0, 1.0, jnp.where(apart == width, -0.5, 0.0))
            return near + jnp.where(apart == UNIT - width, -0.5, 0.0)

        basis[pl.ds(begin, BLOCK), :] = (factor(row_one, one) * factor(row_two, two)).astype(BF16)
        return carry

    lax.fori_loop(0, rows // BLOCK, build_basis, 0)
    pass_on(0)

    target = z * owned + lax.broadcasted_iota(jnp.int32, (owned, lanes), 0)
    found = jnp.zeros((owned, lanes), F32)
    for j in range(pos.shape[0]):
        number = lax.broadcasted_iota(jnp.int32, (1, lanes), 1) + j * lanes
        found = found + jnp.where(pos[j : j + 1, :] == target, number.astype(F32), 0.0)
    own_ids = jnp.sum(found, axis=1, keepdims=True)
    pad = mats.shape[1] - rows - owned
    if pad:
        own_ids = jnp.concatenate([own_ids, jnp.full((pad, 1), -2.0, F32)], axis=0)
    pass_on(1)

    def build_mats(g, carry):
        @pl.when(g != z)
        def _():
            pltpu.make_async_remote_copy(
                src_ref=meta.at[g], dst_ref=meta.at[g], send_sem=meta_send.at[0],
                recv_sem=meta_recv.at[g], device_id={"grid": peers[0]}, device_id_type=MESH,
            ).wait_recv()

        mats[g, rows:, :] = jnp.where(own_ids == meta[g, 4:5, :], 1.0, 0.0).astype(BF16)

        def build(step, inner):
            begin = pl.multiple_of(step * BLOCK, BLOCK)
            row_one, row_two = coords(column(begin, BLOCK), level_one, level_two)
            hat = jnp.maximum(
                1.0 - jnp.abs(row_one.astype(F32) - meta[g, 0:1, :]) * meta[g, 2:3, :], 0.0
            ) * jnp.maximum(
                1.0 - jnp.abs(row_two.astype(F32) - meta[g, 1:2, :]) * meta[g, 3:4, :], 0.0
            )
            mats[g, pl.ds(begin, BLOCK), :] = hat.astype(BF16)
            return inner

        return lax.fori_loop(0, rows // BLOCK, build, carry)

    half = grids // 2
    lax.fori_loop(0, half, build_mats, 0)
    pass_on(2)
    lax.fori_loop(half, grids, build_mats, 0)
    pass_on(3)

    ahead, behind = [], []
    for d in range(4):
        speed = vel[d]
        ahead.append(DIFFUSE - jnp.minimum(speed, 0.0))
        behind.append(DIFFUSE + jnp.maximum(speed, 0.0))
    keep = 1.0
    for d in range(4):
        keep = keep - (ahead[d] + behind[d])

    def power(base, count):
        value = 1.0
        for _ in range(count):
            value = value * base
        return value

    weights = []
    for order in range(1, STEPS + 1):
        table = {}
        for i in range(order + 1):
            weight = (
                float(comb(STEPS, order) * comb(order, i))
                * power(ahead[2], i)
                * power(behind[2], order - i)
            )
            offset = (2 * i - order) % doms
            table[offset] = table[offset] + weight if offset in table else weight
        weights.append(table)

    def store_field(which, begin, value):
        fields[which, pl.ds(UNIT + begin, BLOCK), :] = value

    def wrap(which):
        fields[which, 0:UNIT, :] = fields[which, rows : rows + UNIT, :]
        fields[which, rows + UNIT :, :] = fields[which, UNIT : 2 * UNIT, :]

    def periodic(layer, begin):
        first = pl.multiple_of(lax.rem(begin, rows // 2), BLOCK)
        return jnp.where(
            live == rows, layer[pl.ds(begin, BLOCK), :], layer[pl.ds(first, BLOCK), :]
        )

    def load_start(step, carry):
        begin = pl.multiple_of(step * BLOCK, BLOCK)
        store_field(0, begin, periodic(start, begin))
        return carry

    lax.fori_loop(0, rows // BLOCK, load_start, 0)
    wrap(0)

    for piece in range(PIECES):
        layer_copy(start, sibling, piece, sibling, layer_send.at[0, 0]).wait_recv()
        for slot in sources:
            across = slot + 1 - 2 * core
            layer_copy(start, across, piece, sibling, layer_send.at[0, 0]).wait_recv()

    for order in range(1, STEPS + 1):
        now, later = (order + 1) % 2, order % 2
        table = weights[order - 1]

        def advance(step, carry, now=now, later=later, table=table):
            begin = pl.multiple_of(step * BLOCK, BLOCK)
            at = begin + UNIT
            read = lambda shift: fields[now, pl.ds(at + shift, BLOCK), :]
            centre = read(0)
            along = column(begin, BLOCK) & (stride - 1)
            after = jnp.where(along == stride - 1, read(1 - stride), read(1))
            before = jnp.where(along == 0, read(stride - 1), read(-1))
            value = keep * centre
            value = value + ahead[0] * read(stride) + behind[0] * read(-stride)
            value = value + ahead[1] * after + behind[1] * before
            value = value + ahead[3] * pltpu.roll(centre, lanes - 1, 1)
            value = value + behind[3] * pltpu.roll(centre, 1, 1)
            for offset, weight in table.items():
                source = start if offset == 0 else layers.at[lax.rem(here + offset, doms)]
                value = value + weight * periodic(source, begin)
            store_field(later, begin, value)
            return carry

        lax.fori_loop(0, rows // BLOCK, advance, 0)
        if order < STEPS:
            wrap(later)

    inside = lax.broadcasted_iota(jnp.int32, (rows, 1), 0) < live
    values = jnp.where(inside, fields[STEPS % 2, UNIT : UNIT + rows, :], 0.0)
    weight = coef[0].astype(F32)
    surplus = jnp.where(inside, weight * product(basis[...], values), 0.0)
    surplus_of[z] = surplus

    def surplus_copy(slot, target, send):
        return pltpu.make_async_remote_copy(
            src_ref=surplus_of.at[slot],
            dst_ref=surplus_of.at[slot],
            send_sem=send.at[slot],
            recv_sem=sur_recv.at[slot],
            device_id={"grid": target},
            device_id_type=MESH,
        )

    right, left = jnp.minimum(z + 1, grids - 1), jnp.maximum(z - 1, 0)

    @pl.when(z < grids - 1)
    def _():
        surplus_copy(z, right, right_send).start()

    @pl.when(z > 0)
    def _():
        surplus_copy(z, left, left_send).start()

    total[...] = product(mats[z], surplus)

    def exchange(step, carry):
        low, high = z - step, z + step

        @pl.when(low >= 0)
        def _():
            surplus_copy(low, left, left_send).wait_recv()

            @pl.when(z < grids - 1)
            def _():
                surplus_copy(low, right, right_send).start()

        @pl.when(high < grids)
        def _():
            surplus_copy(high, right, right_send).wait_recv()

            @pl.when(z > 0)
            def _():
                surplus_copy(high, left, left_send).start()

        @pl.when(low >= 0)
        def _():
            total[...] += product(mats[low], surplus_of[low])

        @pl.when(high < grids)
        def _():
            total[...] += product(mats[high], surplus_of[high])

        return carry

    lax.fori_loop(1, grids, exchange, 0)

    own_ref[...] = total[rows : rows + owned, :]
    result_ref[...] = jnp.where(inside, total[0:rows, :], 0.0)

    for piece in range(PIECES):
        for j, peer in enumerate(others):
            layer_copy(start, here, piece, peer, layer_send.at[j, piece]).wait_send()
            layer_copy(start, here, piece, peer, pass_send.at[j, piece]).wait_send()
        layer_copy(start, here, piece, sibling, layer_send.at[chips - 1, piece]).wait_send()
    for j in range(grids - 1):
        meta_copy(j).wait_send()

    def drain(slot, carry):
        @pl.when((z < grids - 1) & (slot <= z))
        def _():
            surplus_copy(slot, right, right_send).wait_send()

        @pl.when((z > 0) & (slot >= z))
        def _():
            surplus_copy(slot, left, left_send).wait_send()

        return carry

    lax.fori_loop(0, grids, drain, 0)


def local(doms, grids, initial, levels, coefficients, velocity, position):
    rows, lanes = initial.shape[1], initial.shape[3]
    owned = position.shape[0] // grids
    padded = -(-owned // 16) * 16
    chips = doms // 2
    vmem = pl.BlockSpec(memory_space=pltpu.VMEM)
    smem = pl.BlockSpec(memory_space=pltpu.SMEM)
    sems = pltpu.SemaphoreType.DMA
    own, result = pl.pallas_call(
        functools.partial(kernel, doms, grids),
        out_shape=[
            jax.ShapeDtypeStruct((owned, lanes), F32),
            jax.ShapeDtypeStruct((rows, lanes), F32),
        ],
        in_specs=[smem, smem, smem, vmem, vmem],
        out_specs=[vmem, vmem],
        scratch_shapes=[
            pltpu.VMEM((doms, rows, lanes), F32),
            pltpu.VMEM((2, rows + 2 * UNIT, lanes), F32),
            pltpu.VMEM((grids, 8, rows), F32),
            pltpu.VMEM((rows, rows), BF16),
            pltpu.VMEM((grids, rows, lanes), F32),
            pltpu.VMEM((grids, rows + padded, rows), BF16),
            pltpu.VMEM((rows + padded, lanes), F32),
            sems((chips, PIECES)),
            sems((doms, PIECES)),
            sems((chips, PIECES)),
            sems((grids,)),
            sems((grids,)),
            sems((grids,)),
            sems((grids,)),
            sems((grids,)),
        ],
        compiler_params=pltpu.CompilerParams(
            collective_id=0, has_side_effects=True, vmem_limit_bytes=48 << 20
        ),
    )(
        levels, coefficients, velocity,
        position.reshape(-1, lanes), initial.reshape(rows, lanes),
    )
    return own[:, None, :], result[None, :, None, :]


def solution(mesh):
    return jax.shard_map(
        functools.partial(local, mesh.shape["dom"], mesh.shape["grid"]),
        mesh=mesh,
        in_specs=(
            P(("parts", "grid"), None, "dom", None),
            P(("parts", "grid"), None),
            P(("parts", "grid")),
            P("parts"),
            P(),
        ),
        out_specs=(P(("parts", "grid"), "dom", None), P(("parts", "grid"), None, "dom", None)),
        check_vma=False,
    )
```

```python
import functools
from math import comb

import jax
import jax.numpy as jnp
from jax import lax
from jax.experimental import pallas as pl
from jax.experimental.pallas import tpu as pltpu
from jax.sharding import PartitionSpec as P

M = 9
LMIN = 2
STEPS = 4
DIFFUSE = 0.05
TOP = M - LMIN
UNIT = 1 << TOP
CHUNKS = 4
HALO = 8
BLOCK = 64
MESH = pl.DeviceIdType.MESH
F32 = jnp.float32
BF16 = jnp.bfloat16


def coords(flat, level_one, level_two):
    one = jnp.left_shift(jnp.right_shift(flat, level_two), TOP - level_one)
    two = jnp.left_shift(flat & (jnp.left_shift(jnp.int32(1), level_two) - 1), TOP - level_two)
    return one, two


def trailing(coord):
    zeros = jnp.zeros_like(coord)
    for bit in range(1, TOP):
        zeros = zeros + jnp.where((coord & ((1 << bit) - 1)) == 0, 1, 0)
    return zeros


def inverse_width(coord, zeros):
    width = jnp.zeros(coord.shape, F32)
    for bit in range(TOP):
        width = jnp.where(zeros == bit, 0.5**bit, width)
    return jnp.where(coord == 0, 0.0, width)


def hier(coord, zeros):
    index = jnp.right_shift(jnp.full_like(coord, UNIT // 2), zeros)
    return jnp.where(coord == 0, 0, index + jnp.right_shift(coord, zeros + 1))


def sparse_ids(one, two, zeros_one, zeros_two):
    h_one, h_two = hier(one, zeros_one), hier(two, zeros_two)
    bits = jnp.where(one == 0, 0, TOP - zeros_one)
    head = jnp.left_shift(jnp.ones_like(one), jnp.maximum(bits - 1, 0))
    low = h_one * (1 << TOP)
    high = (1 << M) + (bits - 1 - LMIN) * (1 << (M - 1)) + (h_one - head) * jnp.left_shift(
        jnp.ones_like(one), M - bits
    )
    return jnp.where(bits <= LMIN, low, high) + h_two


def split(values):
    high = values.astype(BF16)
    low = (values - high.astype(F32)).astype(BF16)
    return jnp.concatenate([high, low], axis=0)


def product(matrix, values):
    width = values.shape[0]
    both = lax.dot_general(
        matrix, split(values), (((1,), (1,)), ((), ())), preferred_element_type=F32
    )
    return both[:, :width] + both[:, width:]


def kernel(
    doms, grids, lev, coef, vel, pos, start, own_ref, result_ref,
    layers, meta, basis, surplus_of, mats, total,
    layer_send, layer_recv, pass_send, meta_send, meta_recv, right_send, left_send, sur_recv,
):
    rows, lanes = start.shape
    owned = own_ref.shape[0]
    chips = doms // 2
    here = lax.axis_index("dom")
    z = lax.axis_index("grid")
    chip, core = here // 2, lax.rem(here, 2)
    sibling = here + 1 - 2 * core
    level_one, level_two = lev[0, 0], lev[0, 1]
    stride, live = jnp.int32(1), jnp.int32(rows)
    for level in range(1, TOP + 1):
        stride = jnp.where(level_two == level, 1 << level, stride)
    for level in range(M):
        live = jnp.where(level_one + level_two == level, 1 << level, live)

    others = [lax.rem(chip + j, chips) * 2 + core for j in range(1, chips)]
    sources = [lax.rem(chip + chips - j, chips) * 2 + core for j in range(1, chips)]
    peers = [lax.rem(z + j, grids) for j in range(1, grids)]

    barrier = pltpu.get_barrier_semaphore()
    for peer in [sibling] + others:
        pl.semaphore_signal(barrier, inc=1, device_id={"dom": peer}, device_id_type=MESH)
    for peer in peers:
        pl.semaphore_signal(barrier, inc=1, device_id={"grid": peer}, device_id_type=MESH)
    pl.semaphore_wait(barrier, chips + grids - 1)

    part = lanes // CHUNKS
    reach = part + 2 * HALO
    whole = jnp.transpose(start[...])
    low_half, high_half = whole[:, : rows // 2], whole[:, rows // 2 :]
    whole = jnp.concatenate([low_half, jnp.where(live == rows, high_half, low_half)], axis=1)
    layers[here, HALO : HALO + lanes, :] = whole
    layers[here, 0:HALO, :] = whole[lanes - HALO :, :]
    layers[here, HALO + lanes :, :] = whole[0:HALO, :]

    def layer_copy(slot, piece, target, send):
        at = pl.ds(0, reach) if piece == 0 else pl.ds(piece * part + 2 * HALO, part)
        return pltpu.make_async_remote_copy(
            src_ref=layers.at[slot, at],
            dst_ref=layers.at[slot, at],
            send_sem=send,
            recv_sem=layer_recv.at[slot, piece],
            device_id={"dom": target},
            device_id_type=MESH,
        )

    for piece in range(CHUNKS):
        for j, peer in enumerate(others):
            layer_copy(here, piece, peer, layer_send.at[j, piece]).start()
    for piece in range(CHUNKS):
        layer_copy(here, piece, sibling, layer_send.at[chips - 1, piece]).start()

    flat = lax.broadcasted_iota(jnp.int32, (1, rows), 1)
    one, two = coords(flat, level_one, level_two)
    zeros_one, zeros_two = trailing(one), trailing(two)
    ids = jnp.where(flat < live, sparse_ids(one, two, zeros_one, zeros_two), -1)
    lines = [
        one.astype(F32), two.astype(F32),
        inverse_width(one, zeros_one), inverse_width(two, zeros_two),
        ids.astype(F32),
    ]
    for line, value in enumerate(lines):
        meta[z, line : line + 1, :] = value
    meta[z, len(lines) :, :] = jnp.zeros((8 - len(lines), rows), F32)

    def meta_copy(j):
        return pltpu.make_async_remote_copy(
            src_ref=meta.at[z],
            dst_ref=meta.at[z],
            send_sem=meta_send.at[j],
            recv_sem=meta_recv.at[z],
            device_id={"grid": peers[j]},
            device_id_type=MESH,
        )

    for j in range(grids - 1):
        meta_copy(j).start()

    def pass_on(piece):
        for j, slot in enumerate(sources):
            layer_copy(slot, piece, sibling, layer_send.at[0, 0]).wait_recv()
            layer_copy(slot, piece, sibling, pass_send.at[j, piece]).start()

    inside = flat < live

    def column(begin, count):
        return begin + lax.broadcasted_iota(jnp.int32, (count, 1), 0)

    def build_basis(step, carry):
        begin = pl.multiple_of(step * BLOCK, BLOCK)
        row_one, row_two = coords(column(begin, BLOCK), level_one, level_two)

        def factor(row, col):
            width = jnp.where(col == 0, 2 * UNIT - 1, col & (-col))
            apart = (row - col) & (UNIT - 1)
            near = jnp.where(apart == 0, 1.0, jnp.where(apart == width, -0.5, 0.0))
            return near + jnp.where(apart == UNIT - width, -0.5, 0.0)

        basis[pl.ds(begin, BLOCK), :] = (factor(row_one, one) * factor(row_two, two)).astype(BF16)
        return carry

    lax.fori_loop(0, rows // BLOCK, build_basis, 0)

    target = z * owned + lax.broadcasted_iota(jnp.int32, (owned, lanes), 0)
    found = jnp.zeros((owned, lanes), F32)
    for j in range(pos.shape[0]):
        number = lax.broadcasted_iota(jnp.int32, (1, lanes), 1) + j * lanes
        found = found + jnp.where(pos[j : j + 1, :] == target, number.astype(F32), 0.0)
    own_ids = jnp.sum(found, axis=1, keepdims=True)
    pad = mats.shape[1] - rows - owned
    if pad:
        own_ids = jnp.concatenate([own_ids, jnp.full((pad, 1), -2.0, F32)], axis=0)

    def build_mats(g, carry):
        @pl.when(g != z)
        def _():
            pltpu.make_async_remote_copy(
                src_ref=meta.at[g], dst_ref=meta.at[g], send_sem=meta_send.at[0],
                recv_sem=meta_recv.at[g], device_id={"grid": peers[0]}, device_id_type=MESH,
            ).wait_recv()

        mats[g, rows:, :] = jnp.where(own_ids == meta[g, 4:5, :], 1.0, 0.0).astype(BF16)

        def build(step, inner):
            begin = pl.multiple_of(step * BLOCK, BLOCK)
            row_one, row_two = coords(column(begin, BLOCK), level_one, level_two)
            hat = jnp.maximum(
                1.0 - jnp.abs(row_one.astype(F32) - meta[g, 0:1, :]) * meta[g, 2:3, :], 0.0
            ) * jnp.maximum(
                1.0 - jnp.abs(row_two.astype(F32) - meta[g, 1:2, :]) * meta[g, 3:4, :], 0.0
            )
            mats[g, pl.ds(begin, BLOCK), :] = hat.astype(BF16)
            return inner

        return lax.fori_loop(0, rows // BLOCK, build, carry)

    ahead, behind = [], []
    for d in range(4):
        speed = vel[d]
        ahead.append(DIFFUSE - jnp.minimum(speed, 0.0))
        behind.append(DIFFUSE + jnp.maximum(speed, 0.0))
    keep = 1.0
    for d in range(4):
        keep = keep - (ahead[d] + behind[d])

    def power(base, count):
        value = 1.0
        for _ in range(count):
            value = value * base
        return value

    weights = []
    for order in range(1, STEPS + 1):
        table = {}
        for i in range(order + 1):
            weight = (
                float(comb(STEPS, order) * comb(order, i))
                * power(ahead[2], i)
                * power(behind[2], order - i)
            )
            offset = (2 * i - order) % doms
            table[offset] = table[offset] + weight if offset in table else weight
        weights.append(table)

    along = flat & (stride - 1)
    first, last = along == 0, along == stride - 1
    weight = coef[0].astype(F32)

    def advance(value):
        shifted = lambda count: pltpu.roll(value, count, 1)
        after = jnp.where(last, shifted(stride - 1), shifted(rows - 1))
        before = jnp.where(first, shifted(rows + 1 - stride), shifted(1))
        moved = keep * value + ahead[1] * after + behind[1] * before
        moved = moved + ahead[0] * shifted(rows - stride) + behind[0] * shifted(stride)
        moved = moved + ahead[3] * pltpu.roll(value, reach - 1, 0)
        return moved + behind[3] * pltpu.roll(value, 1, 0)

    def surplus_part(chunk):
        at = pl.ds(chunk * part, reach)
        value = layers[here, at, :]
        for table in weights:
            value = advance(value)
            for offset, factor in table.items():
                value = value + factor * layers[lax.rem(here + offset, doms), at, :]
        value = jnp.where(inside, value[HALO : HALO + part, :], 0.0)
        both = jnp.dot(split(value), basis[...], preferred_element_type=F32)
        return jnp.where(inside, weight * (both[:part, :] + both[part:, :]), 0.0)

    def surplus_copy(slot, chunk, target, send):
        at = pl.ds(chunk * part, part)
        return pltpu.make_async_remote_copy(
            src_ref=surplus_of.at[slot, at],
            dst_ref=surplus_of.at[slot, at],
            send_sem=send.at[slot, chunk],
            recv_sem=sur_recv.at[slot, chunk],
            device_id={"grid": target},
            device_id_type=MESH,
        )

    right, left = jnp.minimum(z + 1, grids - 1), jnp.maximum(z - 1, 0)

    for chunk in range(CHUNKS):
        pass_on(chunk)
        layer_copy(sibling, chunk, sibling, layer_send.at[0, 0]).wait_recv()
        for slot in sources:
            across = slot + 1 - 2 * core
            layer_copy(across, chunk, sibling, layer_send.at[0, 0]).wait_recv()
        surplus_of[z, chunk * part : (chunk + 1) * part, :] = surplus_part(chunk)

        @pl.when(z < grids - 1)
        def _(chunk=chunk):
            surplus_copy(z, chunk, right, right_send).start()

        @pl.when(z > 0)
        def _(chunk=chunk):
            surplus_copy(z, chunk, left, left_send).start()

        lax.fori_loop(grids * chunk // CHUNKS, grids * (chunk + 1) // CHUNKS, build_mats, 0)

    total[...] = product(mats[z], surplus_of[z])

    def exchange(step, carry):
        low, high = z - step, z + step

        for chunk in range(CHUNKS):

            @pl.when(low >= 0)
            def _(chunk=chunk):
                surplus_copy(low, chunk, left, left_send).wait_recv()

                @pl.when(z < grids - 1)
                def _():
                    surplus_copy(low, chunk, right, right_send).start()

            @pl.when(high < grids)
            def _(chunk=chunk):
                surplus_copy(high, chunk, right, right_send).wait_recv()

                @pl.when(z > 0)
                def _():
                    surplus_copy(high, chunk, left, left_send).start()

        @pl.when(low >= 0)
        def _():
            total[...] += product(mats[low], surplus_of[low])

        @pl.when(high < grids)
        def _():
            total[...] += product(mats[high], surplus_of[high])

        return carry

    lax.fori_loop(1, grids, exchange, 0)

    own_ref[...] = total[rows : rows + owned, :]
    result_ref[...] = jnp.where(
        lax.broadcasted_iota(jnp.int32, (rows, 1), 0) < live, total[0:rows, :], 0.0
    )

    for piece in range(CHUNKS):
        for j, peer in enumerate(others):
            layer_copy(here, piece, peer, layer_send.at[j, piece]).wait_send()
            layer_copy(here, piece, peer, pass_send.at[j, piece]).wait_send()
        layer_copy(here, piece, sibling, layer_send.at[chips - 1, piece]).wait_send()
    for j in range(grids - 1):
        meta_copy(j).wait_send()

    def drain(slot, carry):
        for chunk in range(CHUNKS):

            @pl.when((z < grids - 1) & (slot <= z))
            def _(chunk=chunk):
                surplus_copy(slot, chunk, right, right_send).wait_send()

            @pl.when((z > 0) & (slot >= z))
            def _(chunk=chunk):
                surplus_copy(slot, chunk, left, left_send).wait_send()

        return carry

    lax.fori_loop(0, grids, drain, 0)


def local(doms, grids, initial, levels, coefficients, velocity, position):
    rows, lanes = initial.shape[1], initial.shape[3]
    owned = position.shape[0] // grids
    padded = -(-owned // 16) * 16
    chips = doms // 2
    vmem = pl.BlockSpec(memory_space=pltpu.VMEM)
    smem = pl.BlockSpec(memory_space=pltpu.SMEM)
    sems = pltpu.SemaphoreType.DMA
    own, result = pl.pallas_call(
        functools.partial(kernel, doms, grids),
        out_shape=[
            jax.ShapeDtypeStruct((owned, lanes), F32),
            jax.ShapeDtypeStruct((rows, lanes), F32),
        ],
        in_specs=[smem, smem, smem, vmem, vmem],
        out_specs=[vmem, vmem],
        scratch_shapes=[
            pltpu.VMEM((doms, lanes + 2 * HALO, rows), F32),
            pltpu.VMEM((grids, 8, rows), F32),
            pltpu.VMEM((rows, rows), BF16),
            pltpu.VMEM((grids, lanes, rows), F32),
            pltpu.VMEM((grids, rows + padded, rows), BF16),
            pltpu.VMEM((rows + padded, lanes), F32),
            sems((chips, CHUNKS)),
            sems((doms, CHUNKS)),
            sems((chips, CHUNKS)),
            sems((grids,)),
            sems((grids,)),
            sems((grids, CHUNKS)),
            sems((grids, CHUNKS)),
            sems((grids, CHUNKS)),
        ],
        compiler_params=pltpu.CompilerParams(
            collective_id=0, has_side_effects=True, vmem_limit_bytes=48 << 20
        ),
    )(
        levels, coefficients, velocity,
        position.reshape(-1, lanes), initial.reshape(rows, lanes),
    )
    return own[:, None, :], result[None, :, None, :]


def solution(mesh):
    return jax.shard_map(
        functools.partial(local, mesh.shape["dom"], mesh.shape["grid"]),
        mesh=mesh,
        in_specs=(
            P(("parts", "grid"), None, "dom", None),
            P(("parts", "grid"), None),
            P(("parts", "grid")),
            P("parts"),
            P(),
        ),
        out_specs=(P(("parts", "grid"), "dom", None), P(("parts", "grid"), None, "dom", None)),
        check_vma=False,
    )
```

```python
import functools
from math import comb

import jax
import jax.numpy as jnp
from jax import lax
from jax.experimental import pallas as pl
from jax.experimental.pallas import tpu as pltpu
from jax.sharding import PartitionSpec as P

M = 9
LMIN = 2
STEPS = 4
DIFFUSE = 0.05
TOP = M - LMIN
UNIT = 1 << TOP
SHARES = (4, 4, 4, 4)
CHUNKS = len(SHARES)
STARTS = [sum(SHARES[:c]) for c in range(CHUNKS + 1)]
LAG = 2
HALO = 8
BLOCK = 64
MESH = pl.DeviceIdType.MESH
F32 = jnp.float32
BF16 = jnp.bfloat16


def coords(flat, level_one, level_two):
    one = jnp.left_shift(jnp.right_shift(flat, level_two), TOP - level_one)
    two = jnp.left_shift(flat & (jnp.left_shift(jnp.int32(1), level_two) - 1), TOP - level_two)
    return one, two


def trailing(coord):
    zeros = jnp.zeros_like(coord)
    for bit in range(1, TOP):
        zeros = zeros + jnp.where((coord & ((1 << bit) - 1)) == 0, 1, 0)
    return zeros


def inverse_width(coord, zeros):
    width = jnp.zeros(coord.shape, F32)
    for bit in range(TOP):
        width = jnp.where(zeros == bit, 0.5**bit, width)
    return jnp.where(coord == 0, 0.0, width)


def hier(coord, zeros):
    index = jnp.right_shift(jnp.full_like(coord, UNIT // 2), zeros)
    return jnp.where(coord == 0, 0, index + jnp.right_shift(coord, zeros + 1))


def sparse_ids(one, two, zeros_one, zeros_two):
    h_one, h_two = hier(one, zeros_one), hier(two, zeros_two)
    bits = jnp.where(one == 0, 0, TOP - zeros_one)
    head = jnp.left_shift(jnp.ones_like(one), jnp.maximum(bits - 1, 0))
    low = h_one * (1 << TOP)
    high = (1 << M) + (bits - 1 - LMIN) * (1 << (M - 1)) + (h_one - head) * jnp.left_shift(
        jnp.ones_like(one), M - bits
    )
    return jnp.where(bits <= LMIN, low, high) + h_two


def split(values):
    high = values.astype(BF16)
    low = (values - high.astype(F32)).astype(BF16)
    return jnp.concatenate([high, low], axis=0)


def product(matrix, values):
    width = values.shape[0]
    both = lax.dot_general(
        matrix, split(values), (((1,), (1,)), ((), ())), preferred_element_type=F32
    )
    return both[:, :width] + both[:, width:]


def kernel(
    doms, grids, lev, coef, vel, pos_ref, start_ref, own_ref, result_ref,
    pos, start, layers, meta, basis, surplus_of, mats, total,
    load_sem, layer_send, layer_recv, pass_send, meta_right, meta_left, meta_recv, right_send, left_send, sur_recv,
):
    load_start = pltpu.make_async_copy(start_ref, start, load_sem.at[0])
    load_pos = pltpu.make_async_copy(pos_ref, pos, load_sem.at[1])
    load_start.start()
    load_pos.start()
    rows, lanes = start.shape
    owned = own_ref.shape[0]
    chips = doms // 2
    here = lax.axis_index("dom")
    z = lax.axis_index("grid")
    chip, core = here // 2, lax.rem(here, 2)
    sibling = here + 1 - 2 * core
    level_one, level_two = lev[0, 0], lev[0, 1]
    stride, live = jnp.int32(1), jnp.int32(rows)
    for level in range(1, TOP + 1):
        stride = jnp.where(level_two == level, 1 << level, stride)
    for level in range(M):
        live = jnp.where(level_one + level_two == level, 1 << level, live)

    others = [lax.rem(chip + j, chips) * 2 + core for j in range(1, chips)]
    sources = [lax.rem(chip + chips - j, chips) * 2 + core for j in range(1, chips)]
    right, left = jnp.minimum(z + 1, grids - 1), jnp.maximum(z - 1, 0)
    has_right, has_left = z < grids - 1, z > 0

    barrier = pltpu.get_barrier_semaphore()
    for peer in [sibling] + others:
        pl.semaphore_signal(barrier, inc=1, device_id={"dom": peer}, device_id_type=MESH)

    @pl.when(has_right)
    def _():
        pl.semaphore_signal(barrier, inc=1, device_id={"grid": right}, device_id_type=MESH)

    @pl.when(has_left)
    def _():
        pl.semaphore_signal(barrier, inc=1, device_id={"grid": left}, device_id_type=MESH)

    unit = lanes // STARTS[-1]
    load_start.wait()
    whole = jnp.transpose(start[...])
    low_half, high_half = whole[:, : rows // 2], whole[:, rows // 2 :]
    whole = jnp.concatenate([low_half, jnp.where(live == rows, high_half, low_half)], axis=1)
    layers[here, HALO : HALO + lanes, :] = whole
    layers[here, 0:HALO, :] = whole[lanes - HALO :, :]
    layers[here, HALO + lanes :, :] = whole[0:HALO, :]

    def layer_copy(slot, piece, target, send):
        begin = 2 * HALO if piece else 0
        begin, end = begin + STARTS[piece] * unit, 2 * HALO + STARTS[piece + 1] * unit
        at = pl.ds(begin, end - begin)
        return pltpu.make_async_remote_copy(
            src_ref=layers.at[slot, at],
            dst_ref=layers.at[slot, at],
            send_sem=send,
            recv_sem=layer_recv.at[slot, piece],
            device_id={"dom": target},
            device_id_type=MESH,
        )

    flat = lax.broadcasted_iota(jnp.int32, (1, rows), 1)
    one, two = coords(flat, level_one, level_two)
    zeros_one, zeros_two = trailing(one), trailing(two)
    ids = jnp.where(flat < live, sparse_ids(one, two, zeros_one, zeros_two), -1)
    lines = [
        one.astype(F32), two.astype(F32),
        inverse_width(one, zeros_one), inverse_width(two, zeros_two),
        ids.astype(F32),
    ]
    for line, value in enumerate(lines):
        meta[z, line : line + 1, :] = value
    meta[z, len(lines) :, :] = jnp.zeros((8 - len(lines), rows), F32)

    neighbours = has_right.astype(jnp.int32) + has_left.astype(jnp.int32)
    pl.semaphore_wait(barrier, chips + neighbours)
    for piece in range(CHUNKS):
        for j, peer in enumerate(others):
            layer_copy(here, piece, peer, layer_send.at[j, piece]).start()
    for piece in range(CHUNKS):
        layer_copy(here, piece, sibling, layer_send.at[chips - 1, piece]).start()

    def meta_copy(slot, target, send):
        return pltpu.make_async_remote_copy(
            src_ref=meta.at[slot],
            dst_ref=meta.at[slot],
            send_sem=send.at[slot],
            recv_sem=meta_recv.at[slot],
            device_id={"grid": target},
            device_id_type=MESH,
        )

    @pl.when(has_right)
    def _():
        meta_copy(z, right, meta_right).start()

    @pl.when(has_left)
    def _():
        meta_copy(z, left, meta_left).start()

    def pass_on(piece):
        for j, slot in enumerate(sources):
            layer_copy(slot, piece, sibling, layer_send.at[0, 0]).wait_recv()
            layer_copy(slot, piece, sibling, pass_send.at[j, piece]).start()

    inside = flat < live

    def column(begin, count):
        return begin + lax.broadcasted_iota(jnp.int32, (count, 1), 0)

    def build_basis(step, carry):
        begin = pl.multiple_of(step * BLOCK, BLOCK)
        row_one, row_two = coords(column(begin, BLOCK), level_one, level_two)

        def factor(row, col):
            width = jnp.where(col == 0, 2 * UNIT - 1, col & (-col))
            apart = (row - col) & (UNIT - 1)
            near = jnp.where(apart == 0, 1.0, jnp.where(apart == width, -0.5, 0.0))
            return near + jnp.where(apart == UNIT - width, -0.5, 0.0)

        basis[pl.ds(begin, BLOCK), :] = (factor(row_one, one) * factor(row_two, two)).astype(BF16)
        return carry

    lax.fori_loop(0, rows // BLOCK, build_basis, 0)

    target = z * owned + lax.broadcasted_iota(jnp.int32, (owned, lanes), 0)
    load_pos.wait()
    found = jnp.zeros((owned, lanes), F32)
    for j in range(pos.shape[0]):
        number = lax.broadcasted_iota(jnp.int32, (1, lanes), 1) + j * lanes
        found = found + jnp.where(pos[j : j + 1, :] == target, number.astype(F32), 0.0)
    own_ids = jnp.sum(found, axis=1, keepdims=True)
    pad = mats.shape[1] - rows - owned
    if pad:
        own_ids = jnp.concatenate([own_ids, jnp.full((pad, 1), -2.0, F32)], axis=0)

    def build_mats(g):
        mats[g, rows:, :] = jnp.where(own_ids == meta[g, 4:5, :], 1.0, 0.0).astype(BF16)

        def build(step, inner):
            begin = pl.multiple_of(step * BLOCK, BLOCK)
            row_one, row_two = coords(column(begin, BLOCK), level_one, level_two)
            hat = jnp.maximum(
                1.0 - jnp.abs(row_one.astype(F32) - meta[g, 0:1, :]) * meta[g, 2:3, :], 0.0
            ) * jnp.maximum(
                1.0 - jnp.abs(row_two.astype(F32) - meta[g, 1:2, :]) * meta[g, 3:4, :], 0.0
            )
            mats[g, pl.ds(begin, BLOCK), :] = hat.astype(BF16)
            return inner

        lax.fori_loop(0, rows // BLOCK, build, 0)

    def gather_mats(step, carry):
        low, high = z - step, z + step

        @pl.when(low >= 0)
        def _():
            meta_copy(low, left, meta_left).wait_recv()

            @pl.when(has_right)
            def _():
                meta_copy(low, right, meta_right).start()

        @pl.when(high < grids)
        def _():
            meta_copy(high, right, meta_right).wait_recv()

            @pl.when(has_left)
            def _():
                meta_copy(high, left, meta_left).start()

        @pl.when(low >= 0)
        def _():
            build_mats(low)

        @pl.when(high < grids)
        def _():
            build_mats(high)

        return carry


    ahead, behind = [], []
    for d in range(4):
        speed = vel[d]
        ahead.append(DIFFUSE - jnp.minimum(speed, 0.0))
        behind.append(DIFFUSE + jnp.maximum(speed, 0.0))
    keep = 1.0
    for d in range(4):
        keep = keep - (ahead[d] + behind[d])

    def power(base, count):
        value = 1.0
        for _ in range(count):
            value = value * base
        return value

    weights = []
    for order in range(1, STEPS + 1):
        table = {}
        for i in range(order + 1):
            weight = (
                float(comb(STEPS, order) * comb(order, i))
                * power(ahead[2], i)
                * power(behind[2], order - i)
            )
            offset = (2 * i - order) % doms
            table[offset] = table[offset] + weight if offset in table else weight
        weights.append(table)

    along = flat & (stride - 1)
    first, last = along == 0, along == stride - 1
    weight = coef[0].astype(F32)

    def advance(value):
        shifted = lambda count: pltpu.roll(value, count, 1)
        after = jnp.where(last, shifted(stride - 1), shifted(rows - 1))
        before = jnp.where(first, shifted(rows + 1 - stride), shifted(1))
        moved = keep * value + ahead[1] * after + behind[1] * before
        moved = moved + ahead[0] * shifted(rows - stride) + behind[0] * shifted(stride)
        moved = moved + ahead[3] * pltpu.roll(value, value.shape[0] - 1, 0)
        return moved + behind[3] * pltpu.roll(value, 1, 0)

    def window(chunk):
        return pl.ds(STARTS[chunk] * unit, SHARES[chunk] * unit + 2 * HALO)

    def surplus_part(chunk, value):
        at, part = window(chunk), SHARES[chunk] * unit
        for order, table in enumerate(weights):
            if order:
                value = advance(value)
            for offset, factor in table.items():
                value = value + factor * layers[lax.rem(here + offset, doms), at, :]
        value = jnp.where(inside, value[HALO : HALO + part, :], 0.0)
        both = jnp.dot(split(value), basis[...], preferred_element_type=F32)
        return jnp.where(inside, weight * (both[:part, :] + both[part:, :]), 0.0)

    def surplus_copy(slot, chunk, target, send):
        at = pl.ds(STARTS[chunk] * unit, SHARES[chunk] * unit)
        return pltpu.make_async_remote_copy(
            src_ref=surplus_of.at[slot, at],
            dst_ref=surplus_of.at[slot, at],
            send_sem=send.at[slot, chunk],
            recv_sem=sur_recv.at[slot, chunk],
            device_id={"grid": target},
            device_id_type=MESH,
        )

    def forward(step, chunk):
        low, high = z - step, z + step

        @pl.when(low >= 0)
        def _():
            surplus_copy(low, chunk, left, left_send).wait_recv()

            @pl.when(has_right)
            def _():
                surplus_copy(low, chunk, right, right_send).start()

        @pl.when(high < grids)
        def _():
            surplus_copy(high, chunk, right, right_send).wait_recv()

            @pl.when(has_left)
            def _():
                surplus_copy(high, chunk, left, left_send).start()

    for chunk in range(CHUNKS):
        if chunk == 0:
            pass_on(0)
            build_mats(z)
        value = advance(layers[here, window(chunk), :])
        layer_copy(sibling, chunk, sibling, layer_send.at[0, 0]).wait_recv()
        for slot in sources:
            across = slot + 1 - 2 * core
            layer_copy(across, chunk, sibling, layer_send.at[0, 0]).wait_recv()
        at = pl.ds(STARTS[chunk] * unit, SHARES[chunk] * unit)
        surplus_of[z, at, :] = surplus_part(chunk, value)

        @pl.when(has_right)
        def _(chunk=chunk):
            surplus_copy(z, chunk, right, right_send).start()

        @pl.when(has_left)
        def _(chunk=chunk):
            surplus_copy(z, chunk, left, left_send).start()

        if chunk + 1 < CHUNKS:
            pass_on(chunk + 1)
        if chunk >= LAG:
            forward(1, chunk - LAG)
        begin, end = (max(1, grids * c // CHUNKS) for c in (chunk, chunk + 1))
        if end > begin:
            lax.fori_loop(begin, end, gather_mats, 0)

    for chunk in range(CHUNKS - LAG, CHUNKS):
        forward(1, chunk)
    total[...] = product(mats[z], surplus_of[z])

    def collect(step):
        low, high = z - step, z + step

        @pl.when(low >= 0)
        def _():
            total[...] += product(mats[low], surplus_of[low])

        @pl.when(high < grids)
        def _():
            total[...] += product(mats[high], surplus_of[high])

    def exchange(step, carry):
        collect(step - 1)
        for chunk in range(CHUNKS):
            forward(step, chunk)
        return carry

    lax.fori_loop(2, grids, exchange, 0)
    collect(grids - 1)

    own_ref[...] = total[rows : rows + owned, :]
    result_ref[...] = jnp.where(
        lax.broadcasted_iota(jnp.int32, (rows, 1), 0) < live, total[0:rows, :], 0.0
    )

    for piece in range(CHUNKS):
        for j, peer in enumerate(others):
            layer_copy(here, piece, peer, layer_send.at[j, piece]).wait_send()
            layer_copy(here, piece, peer, pass_send.at[j, piece]).wait_send()
        layer_copy(here, piece, sibling, layer_send.at[chips - 1, piece]).wait_send()
    def drain(slot, carry):
        @pl.when(has_right & (slot <= z))
        def _():
            meta_copy(slot, right, meta_right).wait_send()

        @pl.when(has_left & (slot >= z))
        def _():
            meta_copy(slot, left, meta_left).wait_send()

        for chunk in range(CHUNKS):

            @pl.when(has_right & (slot <= z))
            def _(chunk=chunk):
                surplus_copy(slot, chunk, right, right_send).wait_send()

            @pl.when(has_left & (slot >= z))
            def _(chunk=chunk):
                surplus_copy(slot, chunk, left, left_send).wait_send()

        return carry

    lax.fori_loop(0, grids, drain, 0)


def local(doms, grids, initial, levels, coefficients, velocity, position):
    rows, lanes = initial.shape[1], initial.shape[3]
    owned = position.shape[0] // grids
    padded = -(-owned // 16) * 16
    chips = doms // 2
    vmem = pl.BlockSpec(memory_space=pltpu.VMEM)
    hbm = pl.BlockSpec(memory_space=pltpu.HBM)
    smem = pl.BlockSpec(memory_space=pltpu.SMEM)
    sems = pltpu.SemaphoreType.DMA
    own, result = pl.pallas_call(
        functools.partial(kernel, doms, grids),
        out_shape=[
            jax.ShapeDtypeStruct((owned, lanes), F32),
            jax.ShapeDtypeStruct((rows, lanes), F32),
        ],
        in_specs=[smem, smem, smem, hbm, hbm],
        out_specs=[vmem, vmem],
        scratch_shapes=[
            pltpu.VMEM((position.shape[0] // lanes, lanes), jnp.int32),
            pltpu.VMEM((rows, lanes), F32),
            pltpu.VMEM((doms, lanes + 2 * HALO, rows), F32),
            pltpu.VMEM((grids, 8, rows), F32),
            pltpu.VMEM((rows, rows), BF16),
            pltpu.VMEM((grids, lanes, rows), F32),
            pltpu.VMEM((grids, rows + padded, rows), BF16),
            pltpu.VMEM((rows + padded, lanes), F32),
            sems((2,)),
            sems((chips, CHUNKS)),
            sems((doms, CHUNKS)),
            sems((chips, CHUNKS)),
            sems((grids,)),
            sems((grids,)),
            sems((grids,)),
            sems((grids, CHUNKS)),
            sems((grids, CHUNKS)),
            sems((grids, CHUNKS)),
        ],
        compiler_params=pltpu.CompilerParams(
            collective_id=0, has_side_effects=True, vmem_limit_bytes=48 << 20
        ),
    )(
        levels, coefficients, velocity,
        position.reshape(-1, lanes), initial.reshape(rows, lanes),
    )
    return own[:, None, :], result[None, :, None, :]


def solution(mesh):
    return jax.shard_map(
        functools.partial(local, mesh.shape["dom"], mesh.shape["grid"]),
        mesh=mesh,
        in_specs=(
            P(("parts", "grid"), None, "dom", None),
            P(("parts", "grid"), None),
            P(("parts", "grid")),
            P("parts"),
            P(),
        ),
        out_specs=(P(("parts", "grid"), "dom", None), P(("parts", "grid"), None, "dom", None)),
        check_vma=False,
    )
```

```python
import functools
from math import comb

import jax
import jax.numpy as jnp
from jax import lax
from jax.experimental import pallas as pl
from jax.experimental.pallas import tpu as pltpu
from jax.sharding import PartitionSpec as P

M = 9
LMIN = 2
STEPS = 4
DIFFUSE = 0.05
TOP = M - LMIN
UNIT = 1 << TOP
SHARES = (4, 4, 4, 4)
CHUNKS = len(SHARES)
STARTS = [sum(SHARES[:c]) for c in range(CHUNKS + 1)]
LAG = 2
AHEAD = 2
HALO = 8
BLOCK = 64
MESH = pl.DeviceIdType.MESH
F32 = jnp.float32
BF16 = jnp.bfloat16


def coords(flat, level_one, level_two):
    one = jnp.left_shift(jnp.right_shift(flat, level_two), TOP - level_one)
    two = jnp.left_shift(flat & (jnp.left_shift(jnp.int32(1), level_two) - 1), TOP - level_two)
    return one, two


def trailing(coord):
    zeros = jnp.zeros_like(coord)
    for bit in range(1, TOP):
        zeros = zeros + jnp.where((coord & ((1 << bit) - 1)) == 0, 1, 0)
    return zeros


def inverse_width(coord, zeros):
    width = jnp.zeros(coord.shape, F32)
    for bit in range(TOP):
        width = jnp.where(zeros == bit, 0.5**bit, width)
    return jnp.where(coord == 0, 0.0, width)


def hier(coord, zeros):
    index = jnp.right_shift(jnp.full_like(coord, UNIT // 2), zeros)
    return jnp.where(coord == 0, 0, index + jnp.right_shift(coord, zeros + 1))


def sparse_ids(one, two, zeros_one, zeros_two):
    h_one, h_two = hier(one, zeros_one), hier(two, zeros_two)
    bits = jnp.where(one == 0, 0, TOP - zeros_one)
    head = jnp.left_shift(jnp.ones_like(one), jnp.maximum(bits - 1, 0))
    low = h_one * (1 << TOP)
    high = (1 << M) + (bits - 1 - LMIN) * (1 << (M - 1)) + (h_one - head) * jnp.left_shift(
        jnp.ones_like(one), M - bits
    )
    return jnp.where(bits <= LMIN, low, high) + h_two


def split(values):
    high = values.astype(BF16)
    low = (values - high.astype(F32)).astype(BF16)
    return jnp.concatenate([high, low], axis=0)


def product(matrix, values):
    width = values.shape[0]
    both = lax.dot_general(
        matrix, split(values), (((1,), (1,)), ((), ())), preferred_element_type=F32
    )
    return both[:, :width] + both[:, width:]


def kernel(
    doms, grids, lev, coef, vel, pos_ref, start_ref, own_ref, result_ref,
    pos, start, layers, meta, basis, surplus_of, mats, total,
    load_sem, layer_send, layer_recv, pass_send, meta_right, meta_left, meta_recv, right_send, left_send, sur_recv,
):
    load_start = pltpu.make_async_copy(start_ref, start, load_sem.at[0])
    load_pos = pltpu.make_async_copy(pos_ref, pos, load_sem.at[1])
    load_start.start()
    load_pos.start()
    rows, lanes = start.shape
    owned = own_ref.shape[0]
    chips = doms // 2
    here = lax.axis_index("dom")
    z = lax.axis_index("grid")
    chip, core = here // 2, lax.rem(here, 2)
    sibling = here + 1 - 2 * core
    level_one, level_two = lev[0, 0], lev[0, 1]
    stride, live = jnp.int32(1), jnp.int32(rows)
    for level in range(1, TOP + 1):
        stride = jnp.where(level_two == level, 1 << level, stride)
    for level in range(M):
        live = jnp.where(level_one + level_two == level, 1 << level, live)

    others = [lax.rem(chip + j, chips) * 2 + core for j in range(1, chips)]
    sources = [lax.rem(chip + chips - j, chips) * 2 + core for j in range(1, chips)]
    right, left = jnp.minimum(z + 1, grids - 1), jnp.maximum(z - 1, 0)
    has_right, has_left = z < grids - 1, z > 0

    barrier = pltpu.get_barrier_semaphore()
    for peer in [sibling] + others:
        pl.semaphore_signal(barrier, inc=1, device_id={"dom": peer}, device_id_type=MESH)

    @pl.when(has_right)
    def _():
        pl.semaphore_signal(barrier, inc=1, device_id={"grid": right}, device_id_type=MESH)

    @pl.when(has_left)
    def _():
        pl.semaphore_signal(barrier, inc=1, device_id={"grid": left}, device_id_type=MESH)

    unit = lanes // STARTS[-1]
    load_start.wait()
    whole = jnp.transpose(start[...])
    low_half, high_half = whole[:, : rows // 2], whole[:, rows // 2 :]
    whole = jnp.concatenate([low_half, jnp.where(live == rows, high_half, low_half)], axis=1)
    layers[here, HALO : HALO + lanes, :] = whole
    layers[here, 0:HALO, :] = whole[lanes - HALO :, :]
    layers[here, HALO + lanes :, :] = whole[0:HALO, :]

    def layer_copy(slot, piece, target, send):
        begin = 2 * HALO if piece else 0
        begin, end = begin + STARTS[piece] * unit, 2 * HALO + STARTS[piece + 1] * unit
        at = pl.ds(begin, end - begin)
        return pltpu.make_async_remote_copy(
            src_ref=layers.at[slot, at],
            dst_ref=layers.at[slot, at],
            send_sem=send,
            recv_sem=layer_recv.at[slot, piece],
            device_id={"dom": target},
            device_id_type=MESH,
        )

    flat = lax.broadcasted_iota(jnp.int32, (1, rows), 1)
    one, two = coords(flat, level_one, level_two)
    zeros_one, zeros_two = trailing(one), trailing(two)
    ids = jnp.where(flat < live, sparse_ids(one, two, zeros_one, zeros_two), -1)
    lines = [
        one.astype(F32), two.astype(F32),
        inverse_width(one, zeros_one), inverse_width(two, zeros_two),
        ids.astype(F32),
    ]
    for line, value in enumerate(lines):
        meta[z, line : line + 1, :] = value
    meta[z, len(lines) :, :] = jnp.zeros((8 - len(lines), rows), F32)

    neighbours = has_right.astype(jnp.int32) + has_left.astype(jnp.int32)
    pl.semaphore_wait(barrier, chips + neighbours)
    def send_across(piece):
        for j, peer in enumerate(others):
            layer_copy(here, piece, peer, layer_send.at[j, piece]).start()

    for piece in range(AHEAD):
        send_across(piece)
    for piece in range(CHUNKS):
        layer_copy(here, piece, sibling, layer_send.at[chips - 1, piece]).start()

    def meta_copy(slot, target, send):
        return pltpu.make_async_remote_copy(
            src_ref=meta.at[slot],
            dst_ref=meta.at[slot],
            send_sem=send.at[slot],
            recv_sem=meta_recv.at[slot],
            device_id={"grid": target},
            device_id_type=MESH,
        )

    @pl.when(has_right)
    def _():
        meta_copy(z, right, meta_right).start()

    @pl.when(has_left)
    def _():
        meta_copy(z, left, meta_left).start()

    def pass_on(piece):
        for j, slot in enumerate(sources):
            layer_copy(slot, piece, sibling, layer_send.at[0, 0]).wait_recv()
        if piece + AHEAD < CHUNKS:
            send_across(piece + AHEAD)
        for j, slot in enumerate(sources):
            layer_copy(slot, piece, sibling, pass_send.at[j, piece]).start()

    inside = flat < live

    def column(begin, count):
        return begin + lax.broadcasted_iota(jnp.int32, (count, 1), 0)

    def build_basis(step, carry):
        begin = pl.multiple_of(step * BLOCK, BLOCK)
        row_one, row_two = coords(column(begin, BLOCK), level_one, level_two)

        def factor(row, col):
            width = jnp.where(col == 0, 2 * UNIT - 1, col & (-col))
            apart = (row - col) & (UNIT - 1)
            near = jnp.where(apart == 0, 1.0, jnp.where(apart == width, -0.5, 0.0))
            return near + jnp.where(apart == UNIT - width, -0.5, 0.0)

        basis[pl.ds(begin, BLOCK), :] = (factor(row_one, one) * factor(row_two, two)).astype(BF16)
        return carry

    lax.fori_loop(0, rows // BLOCK, build_basis, 0)

    target = z * owned + lax.broadcasted_iota(jnp.int32, (owned, lanes), 0)
    load_pos.wait()
    found = jnp.zeros((owned, lanes), F32)
    for j in range(pos.shape[0]):
        number = lax.broadcasted_iota(jnp.int32, (1, lanes), 1) + j * lanes
        found = found + jnp.where(pos[j : j + 1, :] == target, number.astype(F32), 0.0)
    own_ids = jnp.sum(found, axis=1, keepdims=True)
    pad = mats.shape[1] - rows - owned
    if pad:
        own_ids = jnp.concatenate([own_ids, jnp.full((pad, 1), -2.0, F32)], axis=0)

    def build_mats(g):
        mats[g, rows:, :] = jnp.where(own_ids == meta[g, 4:5, :], 1.0, 0.0).astype(BF16)

        def build(step, inner):
            begin = pl.multiple_of(step * BLOCK, BLOCK)
            row_one, row_two = coords(column(begin, BLOCK), level_one, level_two)
            hat = jnp.maximum(
                1.0 - jnp.abs(row_one.astype(F32) - meta[g, 0:1, :]) * meta[g, 2:3, :], 0.0
            ) * jnp.maximum(
                1.0 - jnp.abs(row_two.astype(F32) - meta[g, 1:2, :]) * meta[g, 3:4, :], 0.0
            )
            mats[g, pl.ds(begin, BLOCK), :] = hat.astype(BF16)
            return inner

        lax.fori_loop(0, rows // BLOCK, build, 0)

    def gather_mats(step, carry):
        low, high = z - step, z + step

        @pl.when(low >= 0)
        def _():
            meta_copy(low, left, meta_left).wait_recv()

            @pl.when(has_right)
            def _():
                meta_copy(low, right, meta_right).start()

        @pl.when(high < grids)
        def _():
            meta_copy(high, right, meta_right).wait_recv()

            @pl.when(has_left)
            def _():
                meta_copy(high, left, meta_left).start()

        @pl.when(low >= 0)
        def _():
            build_mats(low)

        @pl.when(high < grids)
        def _():
            build_mats(high)

        return carry


    ahead, behind = [], []
    for d in range(4):
        speed = vel[d]
        ahead.append(DIFFUSE - jnp.minimum(speed, 0.0))
        behind.append(DIFFUSE + jnp.maximum(speed, 0.0))
    keep = 1.0
    for d in range(4):
        keep = keep - (ahead[d] + behind[d])

    def power(base, count):
        value = 1.0
        for _ in range(count):
            value = value * base
        return value

    weights = []
    for order in range(1, STEPS + 1):
        table = {}
        for i in range(order + 1):
            weight = (
                float(comb(STEPS, order) * comb(order, i))
                * power(ahead[2], i)
                * power(behind[2], order - i)
            )
            offset = (2 * i - order) % doms
            table[offset] = table[offset] + weight if offset in table else weight
        weights.append(table)

    along = flat & (stride - 1)
    first, last = along == 0, along == stride - 1
    weight = coef[0].astype(F32)

    def advance(value):
        shifted = lambda count: pltpu.roll(value, count, 1)
        after = jnp.where(last, shifted(stride - 1), shifted(rows - 1))
        before = jnp.where(first, shifted(rows + 1 - stride), shifted(1))
        moved = keep * value + ahead[1] * after + behind[1] * before
        moved = moved + ahead[0] * shifted(rows - stride) + behind[0] * shifted(stride)
        moved = moved + ahead[3] * pltpu.roll(value, value.shape[0] - 1, 0)
        return moved + behind[3] * pltpu.roll(value, 1, 0)

    def window(chunk):
        return pl.ds(STARTS[chunk] * unit, SHARES[chunk] * unit + 2 * HALO)

    def surplus_part(chunk, value):
        at, part = window(chunk), SHARES[chunk] * unit
        for order, table in enumerate(weights):
            if order:
                value = advance(value)
            for offset, factor in table.items():
                value = value + factor * layers[lax.rem(here + offset, doms), at, :]
        value = jnp.where(inside, value[HALO : HALO + part, :], 0.0)
        both = jnp.dot(split(value), basis[...], preferred_element_type=F32)
        return jnp.where(inside, weight * (both[:part, :] + both[part:, :]), 0.0)

    def surplus_copy(slot, chunk, target, send):
        at = pl.ds(STARTS[chunk] * unit, SHARES[chunk] * unit)
        return pltpu.make_async_remote_copy(
            src_ref=surplus_of.at[slot, at],
            dst_ref=surplus_of.at[slot, at],
            send_sem=send.at[slot, chunk],
            recv_sem=sur_recv.at[slot, chunk],
            device_id={"grid": target},
            device_id_type=MESH,
        )

    def forward(step, chunk):
        low, high = z - step, z + step

        @pl.when(low >= 0)
        def _():
            surplus_copy(low, chunk, left, left_send).wait_recv()

            @pl.when(has_right)
            def _():
                surplus_copy(low, chunk, right, right_send).start()

        @pl.when(high < grids)
        def _():
            surplus_copy(high, chunk, right, right_send).wait_recv()

            @pl.when(has_left)
            def _():
                surplus_copy(high, chunk, left, left_send).start()

    for chunk in range(CHUNKS):
        if chunk == 0:
            pass_on(0)
            build_mats(z)
        value = advance(layers[here, window(chunk), :])
        layer_copy(sibling, chunk, sibling, layer_send.at[0, 0]).wait_recv()
        for slot in sources:
            across = slot + 1 - 2 * core
            layer_copy(across, chunk, sibling, layer_send.at[0, 0]).wait_recv()
        at = pl.ds(STARTS[chunk] * unit, SHARES[chunk] * unit)
        surplus_of[z, at, :] = surplus_part(chunk, value)

        @pl.when(has_right)
        def _(chunk=chunk):
            surplus_copy(z, chunk, right, right_send).start()

        @pl.when(has_left)
        def _(chunk=chunk):
            surplus_copy(z, chunk, left, left_send).start()

        if chunk + 1 < CHUNKS:
            pass_on(chunk + 1)
        if chunk >= LAG:
            forward(1, chunk - LAG)
        begin, end = (max(1, grids * c // CHUNKS) for c in (chunk, chunk + 1))
        if end > begin:
            lax.fori_loop(begin, end, gather_mats, 0)

    for chunk in range(CHUNKS - LAG, CHUNKS):
        forward(1, chunk)
    total[...] = product(mats[z], surplus_of[z])

    def collect(step):
        low, high = z - step, z + step

        @pl.when(low >= 0)
        def _():
            total[...] += product(mats[low], surplus_of[low])

        @pl.when(high < grids)
        def _():
            total[...] += product(mats[high], surplus_of[high])

    def exchange(step, carry):
        forward(step, 0)
        collect(step - 1)
        for chunk in range(1, CHUNKS):
            forward(step, chunk)
        return carry

    lax.fori_loop(2, grids, exchange, 0)
    collect(grids - 1)

    own_ref[...] = total[rows : rows + owned, :]
    result_ref[...] = jnp.where(
        lax.broadcasted_iota(jnp.int32, (rows, 1), 0) < live, total[0:rows, :], 0.0
    )

    for piece in range(CHUNKS):
        for j, peer in enumerate(others):
            layer_copy(here, piece, peer, layer_send.at[j, piece]).wait_send()
            layer_copy(here, piece, peer, pass_send.at[j, piece]).wait_send()
        layer_copy(here, piece, sibling, layer_send.at[chips - 1, piece]).wait_send()
    def drain(slot, carry):
        @pl.when(has_right & (slot <= z))
        def _():
            meta_copy(slot, right, meta_right).wait_send()

        @pl.when(has_left & (slot >= z))
        def _():
            meta_copy(slot, left, meta_left).wait_send()

        for chunk in range(CHUNKS):

            @pl.when(has_right & (slot <= z))
            def _(chunk=chunk):
                surplus_copy(slot, chunk, right, right_send).wait_send()

            @pl.when(has_left & (slot >= z))
            def _(chunk=chunk):
                surplus_copy(slot, chunk, left, left_send).wait_send()

        return carry

    lax.fori_loop(0, grids, drain, 0)


def local(doms, grids, initial, levels, coefficients, velocity, position):
    rows, lanes = initial.shape[1], initial.shape[3]
    owned = position.shape[0] // grids
    padded = -(-owned // 16) * 16
    chips = doms // 2
    vmem = pl.BlockSpec(memory_space=pltpu.VMEM)
    hbm = pl.BlockSpec(memory_space=pltpu.HBM)
    smem = pl.BlockSpec(memory_space=pltpu.SMEM)
    sems = pltpu.SemaphoreType.DMA
    own, result = pl.pallas_call(
        functools.partial(kernel, doms, grids),
        out_shape=[
            jax.ShapeDtypeStruct((owned, lanes), F32),
            jax.ShapeDtypeStruct((rows, lanes), F32),
        ],
        in_specs=[smem, smem, smem, hbm, hbm],
        out_specs=[vmem, vmem],
        scratch_shapes=[
            pltpu.VMEM((position.shape[0] // lanes, lanes), jnp.int32),
            pltpu.VMEM((rows, lanes), F32),
            pltpu.VMEM((doms, lanes + 2 * HALO, rows), F32),
            pltpu.VMEM((grids, 8, rows), F32),
            pltpu.VMEM((rows, rows), BF16),
            pltpu.VMEM((grids, lanes, rows), F32),
            pltpu.VMEM((grids, rows + padded, rows), BF16),
            pltpu.VMEM((rows + padded, lanes), F32),
            sems((2,)),
            sems((chips, CHUNKS)),
            sems((doms, CHUNKS)),
            sems((chips, CHUNKS)),
            sems((grids,)),
            sems((grids,)),
            sems((grids,)),
            sems((grids, CHUNKS)),
            sems((grids, CHUNKS)),
            sems((grids, CHUNKS)),
        ],
        compiler_params=pltpu.CompilerParams(
            collective_id=0, has_side_effects=True, vmem_limit_bytes=48 << 20
        ),
    )(
        levels, coefficients, velocity,
        position.reshape(-1, lanes), initial.reshape(rows, lanes),
    )
    return own[:, None, :], result[None, :, None, :]


def solution(mesh):
    return jax.shard_map(
        functools.partial(local, mesh.shape["dom"], mesh.shape["grid"]),
        mesh=mesh,
        in_specs=(
            P(("parts", "grid"), None, "dom", None),
            P(("parts", "grid"), None),
            P(("parts", "grid")),
            P("parts"),
            P(),
        ),
        out_specs=(P(("parts", "grid"), "dom", None), P(("parts", "grid"), None, "dom", None)),
        check_vma=False,
    )
```
